1024 devices in a mesh: slab: 128 (over y, z, core), face: 8 (over x).
Axes of the slice: x: 8, y: 8, z: 8, core: 2. Of those that a mesh axis runs over, the one named last changes fastest.
Arguments:
- a_blocks: bfloat16 [8192, 7, 128, 128], P(('slab', 'face')), may hold values from -0.5 to 0.5
- columns: int32 [8192, 7], P(('slab', 'face')), may hold values from 0 to 31
- counts: int32 [8192], P(('slab', 'face')), may hold values from 1 to 7, as said below
- p_blocks: bfloat16 [8192, 128, 128], P(('slab', 'face')), may hold values from -1 to 1
- aggregate: int32 [8192], P(('slab', 'face')), may hold values from 0 to 1
- readers: int32 [1024, 4, 6], P(('slab', 'face')), may hold values from 0 to 7
Outputs:
- coarse: float32 [2048, 5, 2, 128, 128], P(('slab', 'face'))
The draws below stay inside these ranges and needn't reach their ends.
Inputs may be any that keep to these rules, and one draw needn't show every extreme that they name: Each device has some fine row with 7 live slots; devices differ in their typical counts.
All inputs are finite; a program needn't handle non-finite values.
Results may differ from the reference program's by a relative error of at most 0.01.
Values may be sent and summed in bfloat16 or wider, within the bound.
A program may use at most 32 MiB of HBM per device.

```python
import jax
import jax.numpy as jnp
from jax import lax

B = 128
FB = 8
KMAX = 7
RL = 6
CBD = 2
DEVICES_ROWS = 1024
FINE_BLOCKS = 8192
N_SLAB = 128
N_FACE = 8


def draw_counts(key, part):
    key = jax.random.fold_in(key, 7)
    first, second = jax.random.split(key)
    ndev = FINE_BLOCKS // FB
    caps = jax.random.randint(first, (ndev, 1), 2, KMAX + 1)
    values = jax.random.randint(second, (ndev, FB), 1, caps + 1)
    values = values.at[:, 0].set(KMAX)
    return values.reshape(FINE_BLOCKS).astype(jnp.int32)


def plant(values, stream_key, smallest, top_value):
    spot = [jax.random.randint(jax.random.fold_in(stream_key, axis), (), 0, length) for axis, length in enumerate(values.shape)]
    main_axis = values.shape.index(max(values.shape))
    next_to = spot[:main_axis] + [(spot[main_axis] + 1) % values.shape[main_axis]] + spot[main_axis + 1:]
    return values.at[tuple(spot)].set(smallest).at[tuple(next_to)].set(top_value)


def levels(rng, shape, shards, low, largest):
    level = 1.0
    for position, shards_of in shards:
        draws = jax.random.uniform(jax.random.fold_in(jax.random.fold_in(rng, 6), position), (shards_of,), jnp.float32, low / len(shards), largest / len(shards))
        level = level * jnp.repeat(jnp.exp(draws), shape[position] // shards_of).reshape((-1,) + (1,) * (len(shape) - 1 - position))
    return level


def noise(own_key, shape, width, bound, shards=(), kind=jnp.bfloat16):
    drawn = jax.random.normal(own_key, shape, jnp.float32) * width
    if len(shards) > 0:
        drawn = levels(own_key, shape, shards, -0.22, 0.18) * drawn
    return jnp.clip(drawn, min=-bound, max=bound).astype(kind)


def setup_inputs(seed: int = 0) -> dict:
    arg_keys = jax.random.split(jax.random.key(seed), 7)
    a_blocks = noise(arg_keys[0], (FINE_BLOCKS, KMAX, B, B), 0.088, 0.5, ((0, 1024),))
    columns = plant(jax.random.randint(arg_keys[1], (FINE_BLOCKS, KMAX), 0, FB + 4 * RL), jax.random.fold_in(arg_keys[1], 1), 0, (FB + 4 * RL) - 1).astype(jnp.int32)
    counts = draw_counts(jax.random.fold_in(arg_keys[6], 71), 0)
    p_blocks = noise(arg_keys[3], (FINE_BLOCKS, B, B), 0.18, 1.0, ((0, 1024),))
    aggregate = plant(jax.random.randint(arg_keys[4], (FINE_BLOCKS,), 0, CBD), jax.random.fold_in(arg_keys[4], 1), 0, CBD - 1).astype(jnp.int32)
    readers = plant(jax.random.randint(arg_keys[5], (DEVICES_ROWS, 4, RL), 0, FB), jax.random.fold_in(arg_keys[5], 1), 0, FB - 1).astype(jnp.int32)
    return {"a_blocks": a_blocks, "columns": columns, "counts": counts, "p_blocks": p_blocks, "aggregate": aggregate, "readers": readers}


def reference(a_blocks, columns, counts, p_blocks, aggregate, readers):
    ndev = N_SLAB * N_FACE
    a_all = a_blocks.reshape(ndev, FB, KMAX, B, B)
    col_all = columns.reshape(ndev, FB, KMAX)
    cnt_all = counts.reshape(ndev, FB)
    p_all = p_blocks.reshape(ndev, FB, B, B)
    agg_all = aggregate.reshape(ndev, FB)
    groups = 5 * CBD

    def one_device(device):
        slab_at = device // N_FACE
        face_at = device % N_FACE
        neighbours = [
            (device - N_FACE, slab_at >= 1, 1),
            (device + N_FACE, slab_at + 1 < N_SLAB, 0),
            (device - 1, face_at >= 1, 3),
            (device + 1, face_at + 1 < N_FACE, 2),
        ]
        pools = [p_all[device]]
        pool_aggs = [agg_all[device]]
        for other, valid, entry in neighbours:
            other = jnp.clip(other, 0, ndev - 1).astype(jnp.int32)
            listed = readers[other, entry]
            blocks = p_all[other][listed]
            pools.append(jnp.where(valid, blocks, jnp.zeros_like(blocks)))
            pool_aggs.append(agg_all[other][listed])
        pool = jnp.concatenate(pools, axis=0)
        pool_agg = jnp.concatenate(pool_aggs, axis=0)
        cols = col_all[device]
        direction = jnp.where(cols < FB, 0, 1 + (cols - FB) // RL)
        group = direction * CBD + pool_agg[cols]
        live = jnp.arange(KMAX)[None, :] < cnt_all[device][:, None]
        onehot = ((group[..., None] == jnp.arange(groups)[None, None, :]) & live[..., None]).astype(jnp.float32)
        picked = pool[cols].astype(jnp.float32)
        prod = jnp.einsum('ikrs,ikst->ikrt', a_all[device].astype(jnp.float32), picked)
        q_blocks = jnp.einsum('ikg,ikrt->igrt', onehot, prod).astype(jnp.bfloat16)
        z_blocks = jnp.einsum('isr,igst->igrt', p_all[device].astype(jnp.float32), q_blocks.astype(jnp.float32))
        agg_hot = (agg_all[device][:, None] == jnp.arange(CBD)[None, :]).astype(jnp.float32)
        total = jnp.einsum('ia,igrt->agrt', agg_hot, z_blocks)
        return total.reshape(CBD, 5, CBD, B, B)

    result = lax.map(one_device, jnp.arange(ndev, dtype=jnp.int32))
    return result.reshape(ndev * CBD, 5, CBD, B, B)
```

```python
import functools

import jax
import jax.numpy as jnp
from jax import lax
from jax.experimental import pallas as pl
from jax.experimental.pallas import tpu as pltpu
from jax.sharding import PartitionSpec as P

MESH = pl.DeviceIdType.MESH
CBD = 2
FB = 8
KMAX = 7
RL = 6
B = 128
COLS = FB + 4 * RL
SLOTS = FB * KMAX


def neighbours():
    slab, face = lax.axis_index("slab"), lax.axis_index("face")
    n_slab, n_face = lax.axis_size("slab"), lax.axis_size("face")
    return (
        (slab >= 1, (slab - 1, face)),
        (slab + 1 < n_slab, (slab + 1, face)),
        (face >= 1, (slab, face - 1)),
        (face + 1 < n_face, (slab, face + 1)),
    )


def kernel(
    columns, counts, aggregate, readers, a_hbm, p_hbm, out_hbm,
    p, a, send, recv, send_mask, recv_mask, keys, links, table, sums, c, x, out,
    p_sem, a_sem, table_sem, out_sem, send_sem, recv_sem, send_mask_sem, recv_mask_sem,
):
    around = neighbours()
    barrier = pltpu.get_barrier_semaphore()
    for there, device in around:
        @pl.when(there)
        def _():
            pl.semaphore_signal(barrier, inc=1, device_id=device, device_id_type=MESH)

    load_p = pltpu.make_async_copy(p_hbm, p, p_sem)
    load_p.start()
    load_a = [pltpu.make_async_copy(a_hbm.at[i], a.at[i], a_sem.at[i]) for i in range(FB)]
    for copy in load_a:
        copy.start()

    sublane = lax.broadcasted_iota(jnp.int32, (8, B), 0)
    blocks, masks = [], []
    for e in range(4):
        device = around[e][1]
        blocks.append(pltpu.make_async_remote_copy(
            src_ref=send.at[e], dst_ref=recv.at[e ^ 1], send_sem=send_sem.at[e],
            recv_sem=recv_sem.at[e ^ 1], device_id=device, device_id_type=MESH))
        masks.append(pltpu.make_async_remote_copy(
            src_ref=send_mask.at[e], dst_ref=recv_mask.at[e ^ 1], send_sem=send_mask_sem.at[e],
            recv_sem=recv_mask_sem.at[e ^ 1], device_id=device, device_id_type=MESH))
    load_p.wait()
    for n, e in enumerate((2, 3, 0, 1)):
        mask = jnp.zeros((8, B), jnp.int32)
        for r in range(RL):
            block = readers[0, e, r]
            send[e, r] = p[block]
            mask = jnp.where(sublane == r, aggregate[block], mask)
        send_mask[e] = mask.astype(jnp.float32)
        if n == 0:
            expected = sum(there.astype(jnp.int32) for there, unused in around)
            pl.semaphore_wait(barrier, expected)

        @pl.when(around[e][0])
        def _():
            masks[e].start()
            blocks[e].start()

    for i in range(FB):
        for k in range(KMAX):
            key = jnp.where(k < counts[i], aggregate[i] * COLS + columns[i, k], -1)
            m = i * KMAX + k
            keys[m:m + 1, :] = jnp.full((1, B), key, jnp.int32)
    keys[SLOTS:, :] = jnp.full((64 - SLOTS, B), -2, jnp.int32)
    by_row = keys[...]
    row = lax.broadcasted_iota(jnp.int32, (64, B), 0)
    lane = lax.broadcasted_iota(jnp.int32, (64, B), 1)
    by_lane = jnp.sum(jnp.where(row == lane, by_row, 0), axis=0, keepdims=True)
    before = jnp.where((by_row == by_lane) & (row < lane), row + 1, 0)
    links[0:1, :] = jnp.max(before, axis=0, keepdims=True)
    links[1:2, :] = jnp.max(jnp.where(by_row == lane, row + 1, 0), axis=0, keepdims=True)
    links[2:, :] = jnp.zeros((6, B), jnp.int32)
    load_table = pltpu.make_async_copy(links, table, table_sem)
    load_table.start()
    sums[0] = jnp.zeros((B, B), jnp.float32)
    load_table.wait()

    def accumulate(i, carry):
        pltpu.make_async_copy(a_hbm.at[i], a.at[i], a_sem.at[i]).wait()
        wide = jnp.concatenate([a[i, k] for k in range(KMAX)], axis=1)
        product = jnp.dot(p[i].T, wide, preferred_element_type=jnp.float32)
        for k in range(KMAX):
            m = i * KMAX + k
            sums[m + 1] = product[:, k * B:(k + 1) * B] + sums[table[0, m]]
        return carry

    lax.fori_loop(0, FB, accumulate, 0)

    def collect(j, carry):
        c[j, 0:B, :] = sums[table[1, j]].astype(jnp.bfloat16)
        c[j, B:2 * B, :] = sums[table[1, COLS + j]].astype(jnp.bfloat16)
        return carry

    lax.fori_loop(0, COLS, collect, 0)

    stores = []

    def finish(d, first, number):
        left = jnp.concatenate([c[first + j] for j in range(number)], axis=1)
        total = jnp.dot(left, x[0:number * B, :], preferred_element_type=jnp.float32)
        for owner in range(CBD):
            for b in range(CBD):
                out[owner, d, b] = total[owner * B:(owner + 1) * B, b * B:(b + 1) * B]
            store = pltpu.make_async_copy(
                out.at[owner, d], out_hbm.at[owner, d], out_sem.at[owner, d])
            store.start()
            stores.append(store)

    def split(j, block, mask):
        high = block * mask
        x[j * B:(j + 1) * B, B:] = high
        x[j * B:(j + 1) * B, :B] = block - high

    for j in range(FB):
        mask = jnp.full((B, B), aggregate[j], jnp.int32).astype(jnp.float32).astype(jnp.bfloat16)
        split(j, p[j], mask)
    finish(0, 0, FB)

    for q in range(4):
        there = around[q][0]

        @pl.when(there)
        def _():
            blocks[q ^ 1].wait_recv()
            masks[q ^ 1].wait_recv()
            for r in range(RL):
                mask = jnp.broadcast_to(recv_mask[q, r:r + 1, :], (B, B)).astype(jnp.bfloat16)
                split(r, recv[q, r], mask)

        @pl.when(jnp.logical_not(there))
        def _():
            x[0:RL * B, :] = jnp.zeros((RL * B, CBD * B), jnp.bfloat16)

        finish(q + 1, FB + q * RL, RL)

    for store in stores:
        store.wait()
    for e in range(4):
        @pl.when(around[e][0])
        def _():
            masks[e].wait_send()
            blocks[e].wait_send()


def body(a_blocks, columns, counts, p_blocks, aggregate, readers):
    smem = pl.BlockSpec(memory_space=pltpu.SMEM)
    anywhere = pl.BlockSpec(memory_space=pl.ANY)
    bf16, f32, i32 = jnp.bfloat16, jnp.float32, jnp.int32
    return pl.pallas_call(
        kernel,
        out_shape=jax.ShapeDtypeStruct((CBD, 5, CBD, B, B), f32),
        in_specs=[smem] * 4 + [anywhere] * 2,
        out_specs=anywhere,
        scratch_shapes=[
            pltpu.VMEM((FB, B, B), bf16),
            pltpu.VMEM((FB, KMAX, B, B), bf16),
            pltpu.VMEM((4, RL, B, B), bf16),
            pltpu.VMEM((4, RL, B, B), bf16),
            pltpu.VMEM((4, 8, B), f32),
            pltpu.VMEM((4, 8, B), f32),
            pltpu.VMEM((64, B), i32),
            pltpu.VMEM((8, B), i32),
            pltpu.SMEM((8, B), i32),
            pltpu.VMEM((SLOTS + 1, B, B), f32),
            pltpu.VMEM((COLS, CBD * B, B), bf16),
            pltpu.VMEM((FB * B, CBD * B), bf16),
            pltpu.VMEM((CBD, 5, CBD, B, B), f32),
            pltpu.SemaphoreType.DMA,
            pltpu.SemaphoreType.DMA((FB,)),
            pltpu.SemaphoreType.DMA,
            pltpu.SemaphoreType.DMA((CBD, 5)),
            pltpu.SemaphoreType.DMA((4,)),
            pltpu.SemaphoreType.DMA((4,)),
            pltpu.SemaphoreType.DMA((4,)),
            pltpu.SemaphoreType.DMA((4,)),
        ],
        compiler_params=pltpu.CompilerParams(
            collective_id=0, has_side_effects=True, vmem_limit_bytes=40 * 1024 * 1024
        ),
        cost_estimate=pl.CostEstimate(
            flops=700_000_000, bytes_accessed=3_500_000, transcendentals=0
        ),
        name="coarse_blocks",
    )(columns, counts, aggregate, readers, a_blocks, p_blocks)


def solution(mesh):
    in_specs = (
        P(("slab", "face"), None, None, None),
        P(("slab", "face"), None),
        P(("slab", "face")),
        P(("slab", "face"), None, None),
        P(("slab", "face")),
        P(("slab", "face"), None, None),
    )
    out_specs = P(("slab", "face"), None, None, None, None)
    return jax.shard_map(body, mesh=mesh, in_specs=in_specs, out_specs=out_specs, check_vma=False)
```

```python
import functools

import jax
import jax.numpy as jnp
from jax import lax
from jax.experimental import pallas as pl
from jax.experimental.pallas import tpu as pltpu
from jax.sharding import PartitionSpec as P

MESH = pl.DeviceIdType.MESH
CBD = 2
FB = 8
KMAX = 7
RL = 6
B = 128
COLS = FB + 4 * RL
SLOTS = FB * KMAX
LINE = 8


def neighbours():
    slab, face = lax.axis_index("slab"), lax.axis_index("face")
    n_slab, n_face = lax.axis_size("slab"), lax.axis_size("face")
    odd = slab % 2 == 1
    along = (slab // 2) % LINE
    half = n_face // 2
    corner = (slab == 0) & (face == 0)
    beside = (slab == 0) & (face == 1)
    above = (slab == 1) & (face == 0)
    never = slab < 0
    return (
        (slab >= 1, (slab - 1, face), odd | (along == 0),
         (jnp.logical_not(odd) & (along == 0)) | above),
        (slab + 1 < n_slab, (slab + 1, face), odd & (along != LINE - 1), never),
        (face >= 1, (slab, face - 1), (face > half) | beside, beside),
        (face + 1 < n_face, (slab, face + 1), (face < half) & jnp.logical_not(corner), never),
    )


def kernel(
    columns_hbm, counts_hbm, aggregate_hbm, readers_hbm, a_hbm, p_hbm, out,
    columns, counts, aggregate, readers, p, a, send, recv, send_mask, recv_mask, keys, links, table, sums, c, x,
    int_sem, p_sem, a_sem, table_sem, send_sem, recv_sem, send_mask_sem, recv_mask_sem, ready,
):
    around = neighbours()
    load_lists = [
        pltpu.make_async_copy(source, target, int_sem.at[n])
        for n, (source, target) in enumerate((
            (readers_hbm, readers), (aggregate_hbm, aggregate),
            (counts_hbm, counts), (columns_hbm, columns)))
    ]
    load_p = pltpu.make_async_copy(p_hbm, p, p_sem)
    load_a = [pltpu.make_async_copy(a_hbm.at[i], a.at[i], a_sem.at[i]) for i in range(FB)]
    load_lists[0].start()
    load_p.start()
    for copy in load_lists[1:]:
        copy.start()
    barrier = pltpu.get_barrier_semaphore()
    for there, device, later, unused in around:
        @pl.when(there & later)
        def _():
            pl.semaphore_signal(barrier, inc=1, device_id=device, device_id_type=MESH)

    sublane = lax.broadcasted_iota(jnp.int32, (8, B), 0)
    blocks, masks = [], []
    for e in range(4):
        device = around[e][1]
        blocks.append(pltpu.make_async_remote_copy(
            src_ref=send.at[e], dst_ref=recv.at[e ^ 1], send_sem=send_sem.at[e],
            recv_sem=recv_sem.at[e ^ 1], device_id=device, device_id_type=MESH))
        masks.append(pltpu.make_async_remote_copy(
            src_ref=send_mask.at[e], dst_ref=recv_mask.at[e ^ 1], send_sem=send_mask_sem.at[e],
            recv_sem=recv_mask_sem.at[e ^ 1], device_id=device, device_id_type=MESH))

    def pack(e):
        mask = jnp.zeros((8, B), jnp.int32)
        for r in range(RL):
            block = readers[0, e, r]
            send[e, r] = p[block]
            mask = jnp.where(sublane == r, aggregate[block], mask)
        send_mask[e] = mask.astype(jnp.float32)

    def start(e, condition):
        @pl.when(around[e][0] & condition)
        def _():
            masks[e].start()
            blocks[e].start()

    def answer(e, condition):
        there, unused, later, much = around[e]

        @pl.when(there & later & condition)
        def _():
            pl.semaphore_wait(ready.at[e], 1)
            masks[e].start()
            blocks[e].start()

    for copy in load_lists[:2]:
        copy.wait()
    load_p.wait()
    pack(1)
    before = [there & jnp.logical_not(later) for there, unused, later, much in around]
    expected = sum(first.astype(jnp.int32) for first in before)

    @pl.when(expected > 0)
    def _():
        pl.semaphore_wait(barrier, expected)

    start(1, before[1])
    for e in range(4):
        @pl.when(before[e])
        def _():
            pl.semaphore_signal(
                ready.at[e ^ 1], inc=1, device_id=around[e][1], device_id_type=MESH)
    pack(0)
    start(0, before[0])
    pack(2)
    start(2, before[2])
    pack(3)
    start(3, before[3])
    for copy in load_a:
        copy.start()
    for copy in load_lists[2:]:
        copy.wait()

    for i in range(FB):
        for k in range(KMAX):
            key = jnp.where(k < counts[i], aggregate[i] * COLS + columns[i, k], -1)
            m = i * KMAX + k
            keys[m:m + 1, :] = jnp.full((1, B), key, jnp.int32)
    keys[SLOTS:, :] = jnp.full((64 - SLOTS, B), -2, jnp.int32)
    by_row = keys[...]
    row = lax.broadcasted_iota(jnp.int32, (64, B), 0)
    lane = lax.broadcasted_iota(jnp.int32, (64, B), 1)
    by_lane = jnp.sum(jnp.where(row == lane, by_row, 0), axis=0, keepdims=True)
    before = jnp.where((by_row == by_lane) & (row < lane), row + 1, 0)
    links[0:1, :] = jnp.max(before, axis=0, keepdims=True)
    links[1:2, :] = jnp.max(jnp.where(by_row == lane, row + 1, 0), axis=0, keepdims=True)
    links[2:, :] = jnp.zeros((6, B), jnp.int32)
    load_table = pltpu.make_async_copy(links, table, table_sem)
    load_table.start()
    sums[0] = jnp.zeros((B, B), jnp.float32)

    soon = [jnp.logical_not(much) for unused, device, later, much in around]
    answer(0, soon[0])
    answer(3, soon[3])
    answer(2, soon[2])
    load_table.wait()

    def accumulate(i, carry):
        pltpu.make_async_copy(a_hbm.at[i], a.at[i], a_sem.at[i]).wait()
        wide = jnp.concatenate([a[i, k] for k in range(KMAX)], axis=1)
        product = jnp.dot(p[i].T, wide, preferred_element_type=jnp.float32)
        for k in range(KMAX):
            m = i * KMAX + k
            sums[m + 1] = product[:, k * B:(k + 1) * B] + sums[table[0, m]]
        return carry

    lax.fori_loop(0, FB, accumulate, 0)
    answer(1, soon[1])

    def collect(j, carry):
        c[j, 0:B, :] = sums[table[1, j]].astype(jnp.bfloat16)
        c[j, B:2 * B, :] = sums[table[1, COLS + j]].astype(jnp.bfloat16)
        return carry

    lax.fori_loop(0, COLS, collect, 0)

    def finish(d, first, number):
        left = jnp.concatenate([c[first + j] for j in range(number)], axis=1)
        total = jnp.dot(left, x[0:number * B, :], preferred_element_type=jnp.float32)
        for owner in range(CBD):
            for b in range(CBD):
                out[owner, d, b] = total[owner * B:(owner + 1) * B, b * B:(b + 1) * B]

    def split(j, block, mask):
        high = block * mask
        x[j * B:(j + 1) * B, B:] = high
        x[j * B:(j + 1) * B, :B] = block - high

    for j in range(FB):
        mask = jnp.full((B, B), aggregate[j], jnp.int32).astype(jnp.float32).astype(jnp.bfloat16)
        split(j, p[j], mask)
    finish(0, 0, FB)

    for q in (1, 3, 2, 0):
        there = around[q][0]
        if q == 2:
            answer(0, around[0][3])
            answer(2, around[2][3])

        @pl.when(there)
        def _():
            blocks[q ^ 1].wait_recv()
            masks[q ^ 1].wait_recv()
            for r in range(RL):
                mask = jnp.broadcast_to(recv_mask[q, r:r + 1, :], (B, B)).astype(jnp.bfloat16)
                split(r, recv[q, r], mask)

        @pl.when(jnp.logical_not(there))
        def _():
            x[0:RL * B, :] = jnp.zeros((RL * B, CBD * B), jnp.bfloat16)

        finish(q + 1, FB + q * RL, RL)

    for e in range(4):
        @pl.when(around[e][0])
        def _():
            masks[e].wait_send()
            blocks[e].wait_send()


def body(a_blocks, columns, counts, p_blocks, aggregate, readers):
    hbm = pl.BlockSpec(memory_space=pltpu.HBM)
    bf16, f32, i32 = jnp.bfloat16, jnp.float32, jnp.int32
    return pl.pallas_call(
        kernel,
        out_shape=pltpu.VMEM((CBD, 5, CBD, B, B), f32),
        in_specs=[hbm] * 6,
        out_specs=pl.BlockSpec(memory_space=pltpu.VMEM),
        scratch_shapes=[
            pltpu.SMEM((FB, KMAX), i32),
            pltpu.SMEM((FB,), i32),
            pltpu.SMEM((FB,), i32),
            pltpu.SMEM((1, 4, RL), i32),
            pltpu.VMEM((FB, B, B), bf16),
            pltpu.VMEM((FB, KMAX, B, B), bf16),
            pltpu.VMEM((4, RL, B, B), bf16),
            pltpu.VMEM((4, RL, B, B), bf16),
            pltpu.VMEM((4, 8, B), f32),
            pltpu.VMEM((4, 8, B), f32),
            pltpu.VMEM((64, B), i32),
            pltpu.VMEM((8, B), i32),
            pltpu.SMEM((8, B), i32),
            pltpu.VMEM((SLOTS + 1, B, B), f32),
            pltpu.VMEM((COLS, CBD * B, B), bf16),
            pltpu.VMEM((FB * B, CBD * B), bf16),
            pltpu.SemaphoreType.DMA((4,)),
            pltpu.SemaphoreType.DMA,
            pltpu.SemaphoreType.DMA((FB,)),
            pltpu.SemaphoreType.DMA,
            pltpu.SemaphoreType.DMA((4,)),
            pltpu.SemaphoreType.DMA((4,)),
            pltpu.SemaphoreType.DMA((4,)),
            pltpu.SemaphoreType.DMA((4,)),
            pltpu.SemaphoreType.REGULAR((4,)),
        ],
        compiler_params=pltpu.CompilerParams(
            collective_id=0, has_side_effects=True, vmem_limit_bytes=61 * 1024 * 1024
        ),
        cost_estimate=pl.CostEstimate(
            flops=700_000_000, bytes_accessed=3_500_000, transcendentals=0
        ),
        name="coarse_blocks",
    )(columns, counts, aggregate, readers, a_blocks, p_blocks)


def solution(mesh):
    in_specs = (
        P(("slab", "face"), None, None, None),
        P(("slab", "face"), None),
        P(("slab", "face")),
        P(("slab", "face"), None, None),
        P(("slab", "face")),
        P(("slab", "face"), None, None),
    )
    out_specs = P(("slab", "face"), None, None, None, None)
    return jax.shard_map(body, mesh=mesh, in_specs=in_specs, out_specs=out_specs, check_vma=False)
```

```python
import functools

import jax
import jax.numpy as jnp
from jax import lax
from jax.experimental import pallas as pl
from jax.experimental.pallas import tpu as pltpu
from jax.sharding import PartitionSpec as P

MESH = pl.DeviceIdType.MESH
CBD = 2
FB = 8
KMAX = 7
RL = 6
B = 128
COLS = FB + 4 * RL
SLOTS = FB * KMAX
LINE = 8


def neighbours():
    slab, face = lax.axis_index("slab"), lax.axis_index("face")
    n_slab, n_face = lax.axis_size("slab"), lax.axis_size("face")
    odd = slab % 2 == 1
    along = (slab // 2) % LINE
    half = n_face // 2
    corner = (slab == 0) & (face == 0)
    beside = (slab == 0) & (face == 1)
    above = (slab == 1) & (face == 0)
    never = slab < 0
    return (
        (slab >= 1, (slab - 1, face), odd | (along == 0),
         (jnp.logical_not(odd) & (along == 0)) | above),
        (slab + 1 < n_slab, (slab + 1, face), odd & (along != LINE - 1), never),
        (face >= 1, (slab, face - 1), (face > half) | beside, beside),
        (face + 1 < n_face, (slab, face + 1), (face < half) & jnp.logical_not(corner), never),
    )


def spread(row):
    return jnp.broadcast_to(row, (B, B)).astype(jnp.bfloat16)


def split(x, j, block, mask):
    high = block * mask
    x[j * B:(j + 1) * B, B:] = high
    x[j * B:(j + 1) * B, :B] = block - high


def kernel(
    columns_hbm, counts_hbm, aggregate_hbm, readers_hbm, a_hbm, p_hbm,
    out, last, last_blocks, last_mask,
    columns, counts, aggregate, readers, p, a, send, recv, send_mask, recv_mask, keys, links, table, sums, c, x,
    int_sem, p_sem, a_sem, table_sem, send_sem, recv_sem, send_mask_sem, recv_mask_sem, ready,
):
    around = neighbours()
    load_lists = [
        pltpu.make_async_copy(source, target, int_sem.at[n])
        for n, (source, target) in enumerate((
            (readers_hbm, readers), (aggregate_hbm, aggregate),
            (counts_hbm, counts), (columns_hbm, columns)))
    ]
    load_p = pltpu.make_async_copy(p_hbm, p, p_sem)
    load_a = [pltpu.make_async_copy(a_hbm.at[i], a.at[i], a_sem.at[i]) for i in range(FB)]
    load_lists[0].start()
    load_lists[1].start()
    load_p.start()

    barrier = pltpu.get_barrier_semaphore()
    for there, device, later, much in around:
        @pl.when(there & later)
        def _():
            pl.semaphore_signal(barrier, inc=1, device_id=device, device_id_type=MESH)
    before = [there & jnp.logical_not(later) for there, unused, later, much in around]
    expected = sum(first.astype(jnp.int32) for first in before)

    @pl.when(expected > 0)
    def _():
        pl.semaphore_wait(barrier, expected)

    for e in (1, 0, 2, 3):
        @pl.when(before[e])
        def _():
            pl.semaphore_signal(
                ready.at[e ^ 1], inc=1, device_id=around[e][1], device_id_type=MESH)
    for copy in load_lists[2:]:
        copy.start()

    sublane = lax.broadcasted_iota(jnp.int32, (8, B), 0)
    landing = [last_blocks] + [recv.at[n] for n in range(3)]
    landing_mask = [last_mask] + [recv_mask.at[n] for n in range(3)]
    blocks, masks = [], []
    for e in range(4):
        device = around[e][1]
        blocks.append(pltpu.make_async_remote_copy(
            src_ref=send.at[e], dst_ref=landing[e ^ 1], send_sem=send_sem.at[e],
            recv_sem=recv_sem.at[e ^ 1], device_id=device, device_id_type=MESH))
        masks.append(pltpu.make_async_remote_copy(
            src_ref=send_mask.at[e], dst_ref=landing_mask[e ^ 1], send_sem=send_mask_sem.at[e],
            recv_sem=recv_mask_sem.at[e ^ 1], device_id=device, device_id_type=MESH))

    def pack(e):
        mask = jnp.zeros((8, B), jnp.int32)
        for r in range(RL):
            block = readers[0, e, r]
            send[e, r] = p[block]
            mask = jnp.where(sublane == r, aggregate[block], mask)
        send_mask[e] = mask.astype(jnp.float32)

    def start(e, condition):
        @pl.when(around[e][0] & condition)
        def _():
            masks[e].start()
            blocks[e].start()

    def answer(e, condition):
        there, unused, later, much = around[e]

        @pl.when(there & later & condition)
        def _():
            pl.semaphore_wait(ready.at[e], 1)
            masks[e].start()
            blocks[e].start()

    for copy in load_lists[:2]:
        copy.wait()
    load_p.wait()
    for e in (1, 0, 2, 3):
        pack(e)
        start(e, before[e])
    for copy in load_a:
        copy.start()
    for copy in load_lists[2:]:
        copy.wait()

    for i in range(FB):
        for k in range(KMAX):
            key = jnp.where(k < counts[i], aggregate[i] * COLS + columns[i, k], -1)
            m = i * KMAX + k
            keys[m:m + 1, :] = jnp.full((1, B), key, jnp.int32)
    keys[SLOTS:, :] = jnp.full((64 - SLOTS, B), -2, jnp.int32)
    by_row = keys[...]
    row = lax.broadcasted_iota(jnp.int32, (64, B), 0)
    lane = lax.broadcasted_iota(jnp.int32, (64, B), 1)
    by_lane = jnp.sum(jnp.where(row == lane, by_row, 0), axis=0, keepdims=True)
    linked = jnp.where((by_row == by_lane) & (row < lane), row + 1, 0)
    links[0:1, :] = jnp.max(linked, axis=0, keepdims=True)
    links[1:2, :] = jnp.max(jnp.where(by_row == lane, row + 1, 0), axis=0, keepdims=True)
    links[2:, :] = jnp.zeros((6, B), jnp.int32)
    load_table = pltpu.make_async_copy(links, table, table_sem)
    load_table.start()
    sums[0] = jnp.zeros((B, B), jnp.float32)

    soon = [jnp.logical_not(much) for unused, device, later, much in around]
    answer(0, soon[0])
    answer(3, soon[3])
    answer(2, soon[2])
    load_table.wait()

    def accumulate(i, carry):
        pltpu.make_async_copy(a_hbm.at[i], a.at[i], a_sem.at[i]).wait()
        wide = jnp.concatenate([a[i, k] for k in range(KMAX)], axis=1)
        product = jnp.dot(p[i].T, wide, preferred_element_type=jnp.float32)
        for k in range(KMAX):
            m = i * KMAX + k
            sums[m + 1] = product[:, k * B:(k + 1) * B] + sums[table[0, m]]
        return carry

    lax.fori_loop(0, FB, accumulate, 0)
    answer(1, soon[1])

    def collect(j, carry):
        c[j, 0:B, :] = sums[table[1, j]].astype(jnp.bfloat16)
        c[j, B:2 * B, :] = sums[table[1, COLS + j]].astype(jnp.bfloat16)
        return carry

    def collect_last(r, carry):
        last[r, 0:B, :] = sums[table[1, FB + r]].astype(jnp.bfloat16)
        last[r, B:2 * B, :] = sums[table[1, COLS + FB + r]].astype(jnp.bfloat16)
        return carry

    lax.fori_loop(0, FB, collect, 0)
    lax.fori_loop(FB + RL, COLS, collect, 0)
    lax.fori_loop(0, RL, collect_last, 0)

    def finish(d, first, number):
        left = jnp.concatenate([c[first + j] for j in range(number)], axis=1)
        total = jnp.dot(left, x[0:number * B, :], preferred_element_type=jnp.float32)
        for owner in range(CBD):
            for b in range(CBD):
                out[owner, d, b] = total[owner * B:(owner + 1) * B, b * B:(b + 1) * B]

    for j in range(FB):
        mask = jnp.full((B, B), aggregate[j], jnp.int32).astype(jnp.float32).astype(jnp.bfloat16)
        split(x, j, p[j], mask)
    finish(0, 0, FB)

    for q in (1, 3, 2):
        there = around[q][0]
        if q == 2:
            answer(0, around[0][3])
            answer(2, around[2][3])

        @pl.when(there)
        def _():
            blocks[q ^ 1].wait_recv()
            masks[q ^ 1].wait_recv()
            for r in range(RL):
                split(x, r, recv[q - 1, r], spread(recv_mask[q - 1, r:r + 1, :]))

        @pl.when(jnp.logical_not(there))
        def _():
            x[0:RL * B, :] = jnp.zeros((RL * B, CBD * B), jnp.bfloat16)

        finish(q + 1, FB + q * RL, RL)

    there = around[0][0]

    @pl.when(there)
    def _():
        blocks[1].wait_recv()
        masks[1].wait_recv()

    @pl.when(jnp.logical_not(there))
    def _():
        last_blocks[...] = jnp.zeros((RL, B, B), jnp.bfloat16)
        last_mask[...] = jnp.zeros((8, B), jnp.float32)

    for e in range(4):
        @pl.when(around[e][0])
        def _():
            masks[e].wait_send()
            blocks[e].wait_send()


def store_blocks(out, last, last_blocks, last_mask, result, x, piece, out_sem, piece_sem):
    stores = []
    for owner in range(CBD):
        for n, (first, number) in enumerate(((0, 1), (2, 3))):
            there = pl.ds(first, number)
            stores.append(pltpu.make_async_copy(
                out.at[owner, there], result.at[owner, there], out_sem.at[owner, n]))
    for store in stores:
        store.start()
    for r in range(RL):
        split(x, r, last_blocks[r], spread(last_mask[r:r + 1, :]))
    left = jnp.concatenate([last[r] for r in range(RL)], axis=1)
    total = jnp.dot(left, x[...], preferred_element_type=jnp.float32)
    for owner in range(CBD):
        for b in range(CBD):
            piece[owner, b] = total[owner * B:(owner + 1) * B, b * B:(b + 1) * B]
        stores.append(pltpu.make_async_copy(
            piece.at[owner], result.at[owner, 1], piece_sem.at[owner]))
        stores[-1].start()
    for store in stores:
        store.wait()


def body(a_blocks, columns, counts, p_blocks, aggregate, readers):
    hbm = pl.BlockSpec(memory_space=pltpu.HBM)
    vmem = pl.BlockSpec(memory_space=pltpu.VMEM)
    bf16, f32, i32 = jnp.bfloat16, jnp.float32, jnp.int32
    parts = pl.pallas_call(
        kernel,
        out_shape=(
            pltpu.VMEM((CBD, 5, CBD, B, B), f32),
            pltpu.VMEM((RL, CBD * B, B), bf16),
            pltpu.VMEM((RL, B, B), bf16),
            pltpu.VMEM((8, B), f32),
        ),
        in_specs=[hbm] * 6,
        out_specs=(vmem,) * 4,
        scratch_shapes=[
            pltpu.SMEM((FB, KMAX), i32),
            pltpu.SMEM((FB,), i32),
            pltpu.SMEM((FB,), i32),
            pltpu.SMEM((1, 4, RL), i32),
            pltpu.VMEM((FB, B, B), bf16),
            pltpu.VMEM((FB, KMAX, B, B), bf16),
            pltpu.VMEM((4, RL, B, B), bf16),
            pltpu.VMEM((3, RL, B, B), bf16),
            pltpu.VMEM((4, 8, B), f32),
            pltpu.VMEM((3, 8, B), f32),
            pltpu.VMEM((64, B), i32),
            pltpu.VMEM((8, B), i32),
            pltpu.SMEM((8, B), i32),
            pltpu.VMEM((SLOTS + 1, B, B), f32),
            pltpu.VMEM((COLS, CBD * B, B), bf16),
            pltpu.VMEM((FB * B, CBD * B), bf16),
            pltpu.SemaphoreType.DMA((4,)),
            pltpu.SemaphoreType.DMA,
            pltpu.SemaphoreType.DMA((FB,)),
            pltpu.SemaphoreType.DMA,
            pltpu.SemaphoreType.DMA((4,)),
            pltpu.SemaphoreType.DMA((4,)),
            pltpu.SemaphoreType.DMA((4,)),
            pltpu.SemaphoreType.DMA((4,)),
            pltpu.SemaphoreType.REGULAR((4,)),
        ],
        compiler_params=pltpu.CompilerParams(
            collective_id=0, has_side_effects=True, vmem_limit_bytes=60 * 1024 * 1024
        ),
        cost_estimate=pl.CostEstimate(
            flops=700_000_000, bytes_accessed=3_500_000, transcendentals=0
        ),
        name="coarse_blocks",
    )(columns, counts, aggregate, readers, a_blocks, p_blocks)
    return pl.pallas_call(
        store_blocks,
        out_shape=jax.ShapeDtypeStruct((CBD, 5, CBD, B, B), f32),
        in_specs=[vmem] * 4,
        out_specs=hbm,
        scratch_shapes=[
            pltpu.VMEM((RL * B, CBD * B), bf16),
            pltpu.VMEM((CBD, CBD, B, B), f32),
            pltpu.SemaphoreType.DMA((CBD, 2)),
            pltpu.SemaphoreType.DMA((CBD,)),
        ],
        compiler_params=pltpu.CompilerParams(vmem_limit_bytes=8 * 1024 * 1024),
        cost_estimate=pl.CostEstimate(
            flops=100_000_000, bytes_accessed=1_310_720, transcendentals=0
        ),
        name="store_blocks",
    )(*parts)


def solution(mesh):
    in_specs = (
        P(("slab", "face"), None, None, None),
        P(("slab", "face"), None),
        P(("slab", "face")),
        P(("slab", "face"), None, None),
        P(("slab", "face")),
        P(("slab", "face"), None, None),
    )
    out_specs = P(("slab", "face"), None, None, None, None)
    return jax.shard_map(body, mesh=mesh, in_specs=in_specs, out_specs=out_specs, check_vma=False)
```

```python
import functools

import jax
import jax.numpy as jnp
from jax import lax
from jax.experimental import pallas as pl
from jax.experimental.pallas import tpu as pltpu
from jax.sharding import PartitionSpec as P

MESH = pl.DeviceIdType.MESH
CBD = 2
FB = 8
KMAX = 7
RL = 6
B = 128
COLS = FB + 4 * RL
SLOTS = FB * KMAX
LINE = 8


def neighbours():
    slab, face = lax.axis_index("slab"), lax.axis_index("face")
    n_slab, n_face = lax.axis_size("slab"), lax.axis_size("face")
    odd = slab % 2 == 1
    along = (slab // 2) % LINE
    half = n_face // 2
    corner = (slab == 0) & (face == 0)
    beside = (slab == 0) & (face == 1)
    above = (slab == 1) & (face == 0)
    never = slab < 0
    return (
        (slab >= 1, (slab - 1, face), odd | (along == 0),
         (jnp.logical_not(odd) & (along == 0)) | above),
        (slab + 1 < n_slab, (slab + 1, face), odd & (along != LINE - 1), never),
        (face >= 1, (slab, face - 1), (face > half) | beside, beside),
        (face + 1 < n_face, (slab, face + 1), (face < half) & jnp.logical_not(corner), never),
    )


def spread(row):
    return jnp.broadcast_to(row, (B, B)).astype(jnp.bfloat16)


def split(x, j, block, mask):
    high = block * mask
    x[j * B:(j + 1) * B, B:] = high
    x[j * B:(j + 1) * B, :B] = block - high


def kernel(
    columns_hbm, counts_hbm, aggregate_hbm, readers_hbm, a_hbm, p_hbm,
    out, last, last_blocks, last_mask,
    columns, counts, aggregate, readers, p, a, send, recv, send_mask, recv_mask, keys, links, table, sums, c, x,
    int_sem, p_sem, a_sem, table_sem, send_sem, recv_sem, send_mask_sem, recv_mask_sem, ready,
):
    around = neighbours()
    load_lists = [
        pltpu.make_async_copy(source, target, int_sem.at[n])
        for n, (source, target) in enumerate((
            (readers_hbm, readers), (aggregate_hbm, aggregate),
            (counts_hbm, counts), (columns_hbm, columns)))
    ]
    load_p = pltpu.make_async_copy(p_hbm, p, p_sem)
    load_a = [pltpu.make_async_copy(a_hbm.at[i], a.at[i], a_sem.at[i]) for i in range(FB)]
    load_p.start()
    load_lists[0].start()
    load_lists[1].start()

    barrier = pltpu.get_barrier_semaphore()
    for there, device, later, much in around:
        @pl.when(there & later)
        def _():
            pl.semaphore_signal(barrier, inc=1, device_id=device, device_id_type=MESH)
    before = [there & jnp.logical_not(later) for there, unused, later, much in around]
    expected = sum(first.astype(jnp.int32) for first in before)

    @pl.when(expected > 0)
    def _():
        pl.semaphore_wait(barrier, expected)

    for e in (1, 0, 2, 3):
        @pl.when(before[e])
        def _():
            pl.semaphore_signal(
                ready.at[e ^ 1], inc=1, device_id=around[e][1], device_id_type=MESH)
    for copy in load_lists[2:]:
        copy.start()

    sublane = lax.broadcasted_iota(jnp.int32, (8, B), 0)
    landing = [last_blocks] + [recv.at[n] for n in range(3)]
    landing_mask = [last_mask] + [recv_mask.at[n] for n in range(3)]
    blocks, masks = [], []
    for e in range(4):
        device = around[e][1]
        blocks.append(pltpu.make_async_remote_copy(
            src_ref=send.at[e], dst_ref=landing[e ^ 1], send_sem=send_sem.at[e],
            recv_sem=recv_sem.at[e ^ 1], device_id=device, device_id_type=MESH))
        masks.append(pltpu.make_async_remote_copy(
            src_ref=send_mask.at[e], dst_ref=landing_mask[e ^ 1], send_sem=send_mask_sem.at[e],
            recv_sem=recv_mask_sem.at[e ^ 1], device_id=device, device_id_type=MESH))

    def pack(e):
        for r, block in enumerate(listed[e]):
            send[e, r] = p[block]

    def pack_mask(e):
        mask = jnp.zeros((8, B), jnp.int32)
        for r in range(RL):
            mask = jnp.where(sublane == r, aggregate[readers[0, e, r]], mask)
        send_mask[e] = mask.astype(jnp.float32)

    def start_mask(e, condition):
        @pl.when(around[e][0] & condition)
        def _():
            masks[e].start()

    def start(e, condition):
        @pl.when(around[e][0] & condition)
        def _():
            blocks[e].start()

    def answer(e, condition):
        there, unused, later, much = around[e]

        @pl.when(there & later & condition)
        def _():
            pl.semaphore_wait(ready.at[e], 1)
            masks[e].start()
            blocks[e].start()

    for copy in load_lists[:2]:
        copy.wait()
    for e in (1, 0, 2, 3):
        pack_mask(e)
        start_mask(e, before[e])
    listed = [[readers[0, e, r] for r in range(RL)] for e in range(4)]
    load_p.wait()
    for e in (1, 0, 2, 3):
        pack(e)
        start(e, before[e])
    for copy in load_a:
        copy.start()
    for copy in load_lists[2:]:
        copy.wait()

    for i in range(FB):
        for k in range(KMAX):
            key = jnp.where(k < counts[i], aggregate[i] * COLS + columns[i, k], -1)
            m = i * KMAX + k
            keys[m:m + 1, :] = jnp.full((1, B), key, jnp.int32)
    keys[SLOTS:, :] = jnp.full((64 - SLOTS, B), -2, jnp.int32)
    by_row = keys[...]
    row = lax.broadcasted_iota(jnp.int32, (64, B), 0)
    lane = lax.broadcasted_iota(jnp.int32, (64, B), 1)
    by_lane = jnp.sum(jnp.where(row == lane, by_row, 0), axis=0, keepdims=True)
    linked = jnp.where((by_row == by_lane) & (row < lane), row + 1, 0)
    links[0:1, :] = jnp.max(linked, axis=0, keepdims=True)
    links[1:2, :] = jnp.max(jnp.where(by_row == lane, row + 1, 0), axis=0, keepdims=True)
    links[2:, :] = jnp.zeros((6, B), jnp.int32)
    load_table = pltpu.make_async_copy(links, table, table_sem)
    load_table.start()
    sums[0] = jnp.zeros((B, B), jnp.float32)

    soon = [jnp.logical_not(much) for unused, device, later, much in around]
    answer(0, soon[0])
    answer(3, soon[3])
    answer(2, soon[2])
    load_table.wait()

    def accumulate(i, carry):
        pltpu.make_async_copy(a_hbm.at[i], a.at[i], a_sem.at[i]).wait()
        wide = jnp.concatenate([a[i, k] for k in range(KMAX)], axis=1)
        product = jnp.dot(p[i].T, wide, preferred_element_type=jnp.float32)
        for k in range(KMAX):
            m = i * KMAX + k
            sums[m + 1] = product[:, k * B:(k + 1) * B] + sums[table[0, m]]
        return carry

    lax.fori_loop(0, FB, accumulate, 0)
    answer(1, soon[1])

    def collect(j, carry):
        c[j, 0:B, :] = sums[table[1, j]].astype(jnp.bfloat16)
        c[j, B:2 * B, :] = sums[table[1, COLS + j]].astype(jnp.bfloat16)
        return carry

    def collect_last(r, carry):
        last[r, 0:B, :] = sums[table[1, FB + r]].astype(jnp.bfloat16)
        last[r, B:2 * B, :] = sums[table[1, COLS + FB + r]].astype(jnp.bfloat16)
        return carry

    lax.fori_loop(0, FB, collect, 0)
    lax.fori_loop(FB + RL, COLS, collect, 0)
    lax.fori_loop(0, RL, collect_last, 0)

    def finish(d, first, number):
        left = jnp.concatenate([c[first + j] for j in range(number)], axis=1)
        total = jnp.dot(left, x[0:number * B, :], preferred_element_type=jnp.float32)
        for owner in range(CBD):
            for b in range(CBD):
                out[owner, d, b] = total[owner * B:(owner + 1) * B, b * B:(b + 1) * B]

    for j in range(FB):
        mask = jnp.full((B, B), aggregate[j], jnp.int32).astype(jnp.float32).astype(jnp.bfloat16)
        split(x, j, p[j], mask)
    finish(0, 0, FB)

    for q in (1, 3, 2):
        there = around[q][0]
        if q == 2:
            answer(0, around[0][3])
            answer(2, around[2][3])

        @pl.when(there)
        def _():
            blocks[q ^ 1].wait_recv()
            masks[q ^ 1].wait_recv()
            for r in range(RL):
                split(x, r, recv[q - 1, r], spread(recv_mask[q - 1, r:r + 1, :]))

        @pl.when(jnp.logical_not(there))
        def _():
            x[0:RL * B, :] = jnp.zeros((RL * B, CBD * B), jnp.bfloat16)

        finish(q + 1, FB + q * RL, RL)

    for e in range(4):
        @pl.when(around[e][0])
        def _():
            masks[e].wait_send()
            blocks[e].wait_send()

    there = around[0][0]

    @pl.when(there)
    def _():
        blocks[1].wait_recv()
        masks[1].wait_recv()

    @pl.when(jnp.logical_not(there))
    def _():
        last_blocks[...] = jnp.zeros((RL, B, B), jnp.bfloat16)
        last_mask[...] = jnp.zeros((8, B), jnp.float32)


def store_blocks(out, last, last_blocks, last_mask, result, x, piece, out_sem, piece_sem):
    stores = []
    for owner in range(CBD):
        for n, (first, number) in enumerate(((0, 1), (2, 3))):
            there = pl.ds(first, number)
            stores.append(pltpu.make_async_copy(
                out.at[owner, there], result.at[owner, there], out_sem.at[owner, n]))
    for store in stores:
        store.start()
    for r in range(RL):
        split(x, r, last_blocks[r], spread(last_mask[r:r + 1, :]))
    left = jnp.concatenate([last[r] for r in range(RL)], axis=1)
    total = jnp.dot(left, x[...], preferred_element_type=jnp.float32)
    for owner in range(CBD):
        for b in range(CBD):
            piece[owner, b] = total[owner * B:(owner + 1) * B, b * B:(b + 1) * B]
        stores.append(pltpu.make_async_copy(
            piece.at[owner], result.at[owner, 1], piece_sem.at[owner]))
        stores[-1].start()
    for store in stores:
        store.wait()


def body(a_blocks, columns, counts, p_blocks, aggregate, readers):
    hbm = pl.BlockSpec(memory_space=pltpu.HBM)
    vmem = pl.BlockSpec(memory_space=pltpu.VMEM)
    bf16, f32, i32 = jnp.bfloat16, jnp.float32, jnp.int32
    parts = pl.pallas_call(
        kernel,
        out_shape=(
            pltpu.VMEM((CBD, 5, CBD, B, B), f32),
            pltpu.VMEM((RL, CBD * B, B), bf16),
            pltpu.VMEM((RL, B, B), bf16),
            pltpu.VMEM((8, B), f32),
        ),
        in_specs=[hbm] * 6,
        out_specs=(vmem,) * 4,
        scratch_shapes=[
            pltpu.SMEM((FB, KMAX), i32),
            pltpu.SMEM((FB,), i32),
            pltpu.SMEM((FB,), i32),
            pltpu.SMEM((1, 4, RL), i32),
            pltpu.VMEM((FB, B, B), bf16),
            pltpu.VMEM((FB, KMAX, B, B), bf16),
            pltpu.VMEM((4, RL, B, B), bf16),
            pltpu.VMEM((3, RL, B, B), bf16),
            pltpu.VMEM((4, 8, B), f32),
            pltpu.VMEM((3, 8, B), f32),
            pltpu.VMEM((64, B), i32),
            pltpu.VMEM((8, B), i32),
            pltpu.SMEM((8, B), i32),
            pltpu.VMEM((SLOTS + 1, B, B), f32),
            pltpu.VMEM((COLS, CBD * B, B), bf16),
            pltpu.VMEM((FB * B, CBD * B), bf16),
            pltpu.SemaphoreType.DMA((4,)),
            pltpu.SemaphoreType.DMA,
            pltpu.SemaphoreType.DMA((FB,)),
            pltpu.SemaphoreType.DMA,
            pltpu.SemaphoreType.DMA((4,)),
            pltpu.SemaphoreType.DMA((4,)),
            pltpu.SemaphoreType.DMA((4,)),
            pltpu.SemaphoreType.DMA((4,)),
            pltpu.SemaphoreType.REGULAR((4,)),
        ],
        compiler_params=pltpu.CompilerParams(
            collective_id=0, has_side_effects=True, vmem_limit_bytes=60 * 1024 * 1024
        ),
        cost_estimate=pl.CostEstimate(
            flops=700_000_000, bytes_accessed=3_500_000, transcendentals=0
        ),
        name="coarse_blocks",
    )(columns, counts, aggregate, readers, a_blocks, p_blocks)
    return pl.pallas_call(
        store_blocks,
        out_shape=jax.ShapeDtypeStruct((CBD, 5, CBD, B, B), f32),
        in_specs=[vmem] * 4,
        out_specs=hbm,
        scratch_shapes=[
            pltpu.VMEM((RL * B, CBD * B), bf16),
            pltpu.VMEM((CBD, CBD, B, B), f32),
            pltpu.SemaphoreType.DMA((CBD, 2)),
            pltpu.SemaphoreType.DMA((CBD,)),
        ],
        compiler_params=pltpu.CompilerParams(vmem_limit_bytes=8 * 1024 * 1024),
        cost_estimate=pl.CostEstimate(
            flops=100_000_000, bytes_accessed=1_310_720, transcendentals=0
        ),
        name="store_blocks",
    )(*parts)


def solution(mesh):
    in_specs = (
        P(("slab", "face"), None, None, None),
        P(("slab", "face"), None),
        P(("slab", "face")),
        P(("slab", "face"), None, None),
        P(("slab", "face")),
        P(("slab", "face"), None, None),
    )
    out_specs = P(("slab", "face"), None, None, None, None)
    return jax.shard_map(body, mesh=mesh, in_specs=in_specs, out_specs=out_specs, check_vma=False)
```

```python
import functools

import jax
import jax.numpy as jnp
from jax import lax
from jax.experimental import pallas as pl
from jax.experimental.pallas import tpu as pltpu
from jax.sharding import PartitionSpec as P

MESH = pl.DeviceIdType.MESH
CBD = 2
FB = 8
KMAX = 7
RL = 6
B = 128
COLS = FB + 4 * RL
SLOTS = FB * KMAX
LINE = 8
PART = 3


def neighbours():
    slab, face = lax.axis_index("slab"), lax.axis_index("face")
    n_slab, n_face = lax.axis_size("slab"), lax.axis_size("face")
    odd = slab % 2 == 1
    along = (slab // 2) % LINE
    half = n_face // 2
    corner = (slab == 0) & (face == 0)
    beside = (slab == 0) & (face == 1)
    above = (slab == 1) & (face == 0)
    never = slab < 0
    return (
        (slab >= 1, (slab - 1, face), odd | (along == 0),
         (jnp.logical_not(odd) & (along == 0)) | above),
        (slab + 1 < n_slab, (slab + 1, face), odd & (along != LINE - 1), never),
        (face >= 1, (slab, face - 1), (face > half) | beside, beside),
        (face + 1 < n_face, (slab, face + 1), (face < half) & jnp.logical_not(corner), never),
    )


def spread(row):
    return jnp.broadcast_to(row, (B, B)).astype(jnp.bfloat16)


def split(x, j, block, mask):
    high = block * mask
    x[j * B:(j + 1) * B, B:] = high
    x[j * B:(j + 1) * B, :B] = block - high


def kernel(
    columns_hbm, counts_hbm, aggregate_hbm, readers_hbm, a_hbm, p_hbm,
    out, last, last_blocks, last_mask,
    columns, counts, aggregate, readers, p, a, send, recv, send_mask, recv_mask, keys, links, table, sums, c, x,
    int_sem, p_sem, a_sem, table_sem, send_sem, recv_sem, send_mask_sem, recv_mask_sem, ready,
):
    around = neighbours()
    load_lists = [
        pltpu.make_async_copy(source, target, int_sem.at[n])
        for n, (source, target) in enumerate((
            (readers_hbm, readers), (aggregate_hbm, aggregate),
            (counts_hbm, counts), (columns_hbm, columns)))
    ]
    load_p = pltpu.make_async_copy(p_hbm, p, p_sem)
    load_a = [pltpu.make_async_copy(a_hbm.at[i], a.at[i], a_sem.at[i]) for i in range(FB)]
    load_p.start()
    load_lists[0].start()
    load_lists[1].start()

    barrier = pltpu.get_barrier_semaphore()
    for there, device, later, much in around:
        @pl.when(there & later)
        def _():
            pl.semaphore_signal(barrier, inc=1, device_id=device, device_id_type=MESH)
    before = [there & jnp.logical_not(later) for there, unused, later, much in around]
    expected = sum(first.astype(jnp.int32) for first in before)

    @pl.when(expected > 0)
    def _():
        pl.semaphore_wait(barrier, expected)

    for e in (1, 0, 2, 3):
        @pl.when(before[e])
        def _():
            pl.semaphore_signal(
                ready.at[e ^ 1], inc=1, device_id=around[e][1], device_id_type=MESH)
    for copy in load_lists[2:]:
        copy.start()

    sublane = lax.broadcasted_iota(jnp.int32, (8, B), 0)
    landing = [last_blocks] + [recv.at[n] for n in range(3)]
    landing_mask = [last_mask] + [recv_mask.at[n] for n in range(3)]
    blocks, masks = [], []
    for e in range(4):
        device = around[e][1]
        blocks.append(pltpu.make_async_remote_copy(
            src_ref=send.at[e], dst_ref=landing[e ^ 1], send_sem=send_sem.at[e],
            recv_sem=recv_sem.at[e ^ 1], device_id=device, device_id_type=MESH))
        masks.append(pltpu.make_async_remote_copy(
            src_ref=send_mask.at[e], dst_ref=landing_mask[e ^ 1], send_sem=send_mask_sem.at[e],
            recv_sem=recv_mask_sem.at[e ^ 1], device_id=device, device_id_type=MESH))

    def pack(e):
        for r, block in enumerate(listed[e]):
            send[e, r] = p[block]

    def pack_mask(e):
        mask = jnp.zeros((8, B), jnp.int32)
        for r in range(RL):
            mask = jnp.where(sublane == r, aggregate[readers[0, e, r]], mask)
        send_mask[e] = mask.astype(jnp.float32)

    def start_mask(e, condition):
        @pl.when(around[e][0] & condition)
        def _():
            masks[e].start()

    def start(e, condition):
        @pl.when(around[e][0] & condition)
        def _():
            blocks[e].start()

    def answer(e, condition):
        there, unused, later, much = around[e]

        @pl.when(there & later & condition)
        def _():
            pl.semaphore_wait(ready.at[e], 1)
            masks[e].start()
            blocks[e].start()

    for copy in load_lists[:2]:
        copy.wait()
    for e in (1, 0, 2, 3):
        pack_mask(e)
        start_mask(e, before[e])
    listed = [[readers[0, e, r] for r in range(RL)] for e in range(4)]
    load_p.wait()
    for r in range(0, RL, PART):
        for block in range(r, r + PART):
            send[1, block] = p[listed[1][block]]

        @pl.when(before[1])
        def _():
            pltpu.make_async_remote_copy(
                src_ref=send.at[1, pl.ds(r, PART)], dst_ref=last_blocks.at[pl.ds(r, PART)],
                send_sem=send_sem.at[1], recv_sem=recv_sem.at[0],
                device_id=around[1][1], device_id_type=MESH).start()

    for e in (0, 2, 3):
        pack(e)
        start(e, before[e])
    for copy in load_a:
        copy.start()
    for copy in load_lists[2:]:
        copy.wait()

    for i in range(FB):
        for k in range(KMAX):
            key = jnp.where(k < counts[i], aggregate[i] * COLS + columns[i, k], -1)
            m = i * KMAX + k
            keys[m:m + 1, :] = jnp.full((1, B), key, jnp.int32)
    keys[SLOTS:, :] = jnp.full((64 - SLOTS, B), -2, jnp.int32)
    by_row = keys[...]
    row = lax.broadcasted_iota(jnp.int32, (64, B), 0)
    lane = lax.broadcasted_iota(jnp.int32, (64, B), 1)
    by_lane = jnp.sum(jnp.where(row == lane, by_row, 0), axis=0, keepdims=True)
    linked = jnp.where((by_row == by_lane) & (row < lane), row + 1, 0)
    links[0:1, :] = jnp.max(linked, axis=0, keepdims=True)
    links[1:2, :] = jnp.max(jnp.where(by_row == lane, row + 1, 0), axis=0, keepdims=True)
    links[2:, :] = jnp.zeros((6, B), jnp.int32)
    load_table = pltpu.make_async_copy(links, table, table_sem)
    load_table.start()
    sums[0] = jnp.zeros((B, B), jnp.float32)

    soon = [jnp.logical_not(much) for unused, device, later, much in around]
    answer(0, soon[0])
    answer(3, soon[3])
    answer(2, soon[2])
    load_table.wait()

    def accumulate(i, carry):
        pltpu.make_async_copy(a_hbm.at[i], a.at[i], a_sem.at[i]).wait()
        wide = jnp.concatenate([a[i, k] for k in range(KMAX)], axis=1)
        product = jnp.dot(p[i].T, wide, preferred_element_type=jnp.float32)
        for k in range(KMAX):
            m = i * KMAX + k
            sums[m + 1] = product[:, k * B:(k + 1) * B] + sums[table[0, m]]
        return carry

    lax.fori_loop(0, FB, accumulate, 0)
    answer(1, soon[1])

    def collect(j, carry):
        c[j, 0:B, :] = sums[table[1, j]].astype(jnp.bfloat16)
        c[j, B:2 * B, :] = sums[table[1, COLS + j]].astype(jnp.bfloat16)
        return carry

    def collect_last(r, carry):
        last[r, 0:B, :] = sums[table[1, FB + r]].astype(jnp.bfloat16)
        last[r, B:2 * B, :] = sums[table[1, COLS + FB + r]].astype(jnp.bfloat16)
        return carry

    lax.fori_loop(0, FB, collect, 0)
    lax.fori_loop(FB + RL, COLS, collect, 0)
    lax.fori_loop(0, RL, collect_last, 0)

    def finish(d, first, number):
        left = jnp.concatenate([c[first + j] for j in range(number)], axis=1)
        total = jnp.dot(left, x[0:number * B, :], preferred_element_type=jnp.float32)
        for owner in range(CBD):
            for b in range(CBD):
                out[owner, d, b] = total[owner * B:(owner + 1) * B, b * B:(b + 1) * B]

    for j in range(FB):
        mask = jnp.full((B, B), aggregate[j], jnp.int32).astype(jnp.float32).astype(jnp.bfloat16)
        split(x, j, p[j], mask)
    finish(0, 0, FB)

    for q in (1, 3, 2):
        there = around[q][0]
        if q == 2:
            answer(0, around[0][3])
            answer(2, around[2][3])

        @pl.when(there)
        def _():
            blocks[q ^ 1].wait_recv()
            masks[q ^ 1].wait_recv()
            for r in range(RL):
                split(x, r, recv[q - 1, r], spread(recv_mask[q - 1, r:r + 1, :]))

        @pl.when(jnp.logical_not(there))
        def _():
            x[0:RL * B, :] = jnp.zeros((RL * B, CBD * B), jnp.bfloat16)

        finish(q + 1, FB + q * RL, RL)

    for e in range(4):
        @pl.when(around[e][0])
        def _():
            masks[e].wait_send()
            blocks[e].wait_send()

    there = around[0][0]

    @pl.when(there)
    def _():
        blocks[1].wait_recv()
        masks[1].wait_recv()

    @pl.when(jnp.logical_not(there))
    def _():
        last_blocks[...] = jnp.zeros((RL, B, B), jnp.bfloat16)
        last_mask[...] = jnp.zeros((8, B), jnp.float32)


def store_blocks(out, last, last_blocks, last_mask, result, x, piece, out_sem, piece_sem):
    stores = []
    for owner in range(CBD):
        for n, (first, number) in enumerate(((0, 1), (2, 3))):
            there = pl.ds(first, number)
            stores.append(pltpu.make_async_copy(
                out.at[owner, there], result.at[owner, there], out_sem.at[owner, n]))
    for store in stores:
        store.start()
    for r in range(RL):
        split(x, r, last_blocks[r], spread(last_mask[r:r + 1, :]))
    left = jnp.concatenate([last[r] for r in range(RL)], axis=1)
    total = jnp.dot(left, x[...], preferred_element_type=jnp.float32)
    for owner in range(CBD):
        for b in range(CBD):
            piece[owner, b] = total[owner * B:(owner + 1) * B, b * B:(b + 1) * B]
        stores.append(pltpu.make_async_copy(
            piece.at[owner], result.at[owner, 1], piece_sem.at[owner]))
        stores[-1].start()
    for store in stores:
        store.wait()


def body(a_blocks, columns, counts, p_blocks, aggregate, readers):
    hbm = pl.BlockSpec(memory_space=pltpu.HBM)
    vmem = pl.BlockSpec(memory_space=pltpu.VMEM)
    bf16, f32, i32 = jnp.bfloat16, jnp.float32, jnp.int32
    parts = pl.pallas_call(
        kernel,
        out_shape=(
            pltpu.VMEM((CBD, 5, CBD, B, B), f32),
            pltpu.VMEM((RL, CBD * B, B), bf16),
            pltpu.VMEM((RL, B, B), bf16),
            pltpu.VMEM((8, B), f32),
        ),
        in_specs=[hbm] * 6,
        out_specs=(vmem,) * 4,
        scratch_shapes=[
            pltpu.SMEM((FB, KMAX), i32),
            pltpu.SMEM((FB,), i32),
            pltpu.SMEM((FB,), i32),
            pltpu.SMEM((1, 4, RL), i32),
            pltpu.VMEM((FB, B, B), bf16),
            pltpu.VMEM((FB, KMAX, B, B), bf16),
            pltpu.VMEM((4, RL, B, B), bf16),
            pltpu.VMEM((3, RL, B, B), bf16),
            pltpu.VMEM((4, 8, B), f32),
            pltpu.VMEM((3, 8, B), f32),
            pltpu.VMEM((64, B), i32),
            pltpu.VMEM((8, B), i32),
            pltpu.SMEM((8, B), i32),
            pltpu.VMEM((SLOTS + 1, B, B), f32),
            pltpu.VMEM((COLS, CBD * B, B), bf16),
            pltpu.VMEM((FB * B, CBD * B), bf16),
            pltpu.SemaphoreType.DMA((4,)),
            pltpu.SemaphoreType.DMA,
            pltpu.SemaphoreType.DMA((FB,)),
            pltpu.SemaphoreType.DMA,
            pltpu.SemaphoreType.DMA((4,)),
            pltpu.SemaphoreType.DMA((4,)),
            pltpu.SemaphoreType.DMA((4,)),
            pltpu.SemaphoreType.DMA((4,)),
            pltpu.SemaphoreType.REGULAR((4,)),
        ],
        compiler_params=pltpu.CompilerParams(
            collective_id=0, has_side_effects=True, vmem_limit_bytes=60 * 1024 * 1024
        ),
        cost_estimate=pl.CostEstimate(
            flops=700_000_000, bytes_accessed=3_500_000, transcendentals=0
        ),
        name="coarse_blocks",
    )(columns, counts, aggregate, readers, a_blocks, p_blocks)
    return pl.pallas_call(
        store_blocks,
        out_shape=jax.ShapeDtypeStruct((CBD, 5, CBD, B, B), f32),
        in_specs=[vmem] * 4,
        out_specs=hbm,
        scratch_shapes=[
            pltpu.VMEM((RL * B, CBD * B), bf16),
            pltpu.VMEM((CBD, CBD, B, B), f32),
            pltpu.SemaphoreType.DMA((CBD, 2)),
            pltpu.SemaphoreType.DMA((CBD,)),
        ],
        compiler_params=pltpu.CompilerParams(vmem_limit_bytes=8 * 1024 * 1024),
        cost_estimate=pl.CostEstimate(
            flops=100_000_000, bytes_accessed=1_310_720, transcendentals=0
        ),
        name="store_blocks",
    )(*parts)


def solution(mesh):
    in_specs = (
        P(("slab", "face"), None, None, None),
        P(("slab", "face"), None),
        P(("slab", "face")),
        P(("slab", "face"), None, None),
        P(("slab", "face")),
        P(("slab", "face"), None, None),
    )
    out_specs = P(("slab", "face"), None, None, None, None)
    return jax.shard_map(body, mesh=mesh, in_specs=in_specs, out_specs=out_specs, check_vma=False)
```
